32 devices in a mesh: groups: 2 (over y), ctx: 4 (over z), head: 2 (over x), feat: 2 (over core).
Axes of the slice: x: 2, y: 2, z: 4, core: 2. Of those that a mesh axis runs over, the one named last changes fastest.
Arguments:
- queries: bfloat16 [1024, 5120], P(('groups', 'ctx'), 'head'), parts along dimension 0, may hold values from -6 to 6
- keys: bfloat16 [1024, 1024], P(('groups', 'ctx'), 'head'), parts along dimension 0, may hold values from -6 to 6
- values: bfloat16 [1024, 1024], P(('groups', 'ctx'), 'head'), parts along dimension 0, may hold values from -6 to 6
- log_gate: float32 [1024, 8], P(('groups', 'ctx'), 'head'), parts along dimension 0, may hold values from -1 to 0, as said below
- cand_q: bfloat16 [128, 5120], P('groups', 'head'), parts along dimension 0, may hold values from -12 to 12
- cand_kv: bfloat16 [128, 2, 1024], P('groups', None, 'head'), parts along dimension 0, may hold values from -12 to 12
- token_ids: int32 [32], P('groups'), parts along dimension 0, may hold values from 0 to 63
- fork_pos: int32 [32], P('groups'), parts along dimension 0, may hold values from 1 to 4
- slot_map: int32 [32], P('groups'), parts along dimension 0, may hold values from 0 to 15, each once
Outputs:
- prefill_out: bfloat16 [1024, 5120], P(('groups', 'ctx', 'feat'), 'head'), parts along dimension 0
- branch_out: bfloat16 [32, 5120], P(('groups', 'ctx', 'feat'), 'head'), parts along dimension 0
The draws below stay inside these ranges and needn't reach their ends.
There are 2 independent parts, one for each index of `groups`. The reference program is written for one: setup_inputs(seed, part) draws one part's arguments, and reference() takes and returns one part's arrays. A program takes and returns all parts, laid end to end along the dimension named above; each array names one. Nothing has to cross between parts.
Inputs may be any that keep to these rules, and one draw needn't show every extreme that they name: log_gate is never positive.
All inputs are finite; a program needn't handle non-finite values.
Results may differ from the reference program's by a relative error of at most 0.0055.
Values may be sent and summed in bfloat16 or wider, within the bound.
A program may use at most 192 MiB of HBM per device.

```python
import math
import jax
import jax.numpy as jnp
import numpy as np
from jax import lax

HEAD = 128
QHEADS = 40
LOOKUP_GROUPS = 8
TOK_DEV = 128
CANDS = 64
GROUP = 5
FEATS = 8256
CONTEXT_LENGTH = 512
BRANCHES = 16
N_CTX = 4


def draw_log_gate(key, part):
    complete_lookup_vectors = jax.random.split(key, 7)
    blocks = CONTEXT_LENGTH // TOK_DEV
    fast_share = 0.5
    fast = jax.random.uniform(complete_lookup_vectors[0], (LOOKUP_GROUPS,), jnp.float32) < fast_share
    fast_rate = 1.0 / jax.random.uniform(complete_lookup_vectors[1], (LOOKUP_GROUPS,), jnp.float32, 30.0, 50.0)
    slow_rate = jax.random.uniform(complete_lookup_vectors[2], (LOOKUP_GROUPS,), jnp.float32, 0.1, 0.8) / CONTEXT_LENGTH
    base = jnp.where(fast, fast_rate, slow_rate)
    block_factor = jnp.exp(jax.random.uniform(complete_lookup_vectors[3], (blocks, 1, LOOKUP_GROUPS), jnp.float32, -0.7, 0.7))
    jitter = jax.random.uniform(complete_lookup_vectors[4], (blocks, TOK_DEV, LOOKUP_GROUPS), jnp.float32, 0.5, 1.5)
    forgetting_speed = (base[None, None, :] * block_factor * jitter).reshape(CONTEXT_LENGTH, LOOKUP_GROUPS)
    sampled_item_lines = jax.random.randint(complete_lookup_vectors[5], (2, LOOKUP_GROUPS), 0, CONTEXT_LENGTH)
    sequence_places = jnp.arange(CONTEXT_LENGTH)[:, None, None]
    causal_allowance = jnp.any(sequence_places == sampled_item_lines[None, :, :], axis=1)
    decoded_item_group = jnp.log(jax.random.uniform(complete_lookup_vectors[6], (CONTEXT_LENGTH, LOOKUP_GROUPS), jnp.float32, 0.5, 0.8))
    return (-forgetting_speed + jnp.where(causal_allowance, decoded_item_group, 0.0)).astype(jnp.float32)


def touch_ends(values, rng, low, largest):
    place = [jax.random.randint(jax.random.fold_in(rng, axis), (), 0, length) for axis, length in enumerate(values.shape)]
    main_axis = values.shape.index(max(values.shape))
    beside = place[:main_axis] + [(place[main_axis] + 1) % values.shape[main_axis]] + place[main_axis + 1:]
    return values.at[tuple(place)].set(low).at[tuple(beside)].set(largest)


def block_levels(key, dims, cuts, low, high):
    def one(axis_at, shards_of):
        heights = jax.random.uniform(jax.random.fold_in(jax.random.fold_in(key, 6), axis_at), (shards_of,), jnp.float32, low / len(cuts), high / len(cuts))
        return jnp.repeat(jnp.exp(heights), dims[axis_at] // shards_of).reshape((-1,) + (1,) * (len(dims) - axis_at - 1))

    level = one(*cuts[0])
    for cut in cuts[1:]:
        level = level * one(*cut)
    return level


def bell_draw(own_key, dims, scale, reach, cuts=(), kind=jnp.bfloat16):
    result = jax.random.normal(own_key, dims, jnp.float32) * scale
    if len(cuts) > 0:
        result = block_levels(own_key, dims, cuts, -0.22, 0.18) * result
    return jnp.clip(result, min=-reach, max=reach).astype(kind)


def setup_inputs(seed: int = 0, part: int = 0) -> dict:
    seeds = jax.random.split(jax.random.key(seed), 10)
    part_keys = jax.random.split(jax.random.fold_in(seeds[9], part), 10)
    return {
        "queries": bell_draw(part_keys[0], (CONTEXT_LENGTH, QHEADS * HEAD), 1.0, 6.0, ((0, 4), (1, 2))),
        "keys": bell_draw(part_keys[1], (CONTEXT_LENGTH, LOOKUP_GROUPS * HEAD), 1.0, 6.0, ((0, 4), (1, 2))),
        "values": bell_draw(part_keys[2], (CONTEXT_LENGTH, LOOKUP_GROUPS * HEAD), 1.0, 6.0, ((0, 4), (1, 2))),
        "log_gate": draw_log_gate(jax.random.fold_in(jax.random.fold_in(seeds[9], part), 71), part),
        "cand_q": bell_draw(part_keys[4], (CANDS, QHEADS * HEAD), 2.0, 12.0, ((1, 2),)),
        "cand_kv": bell_draw(part_keys[5], (CANDS, 2, LOOKUP_GROUPS * HEAD), 2.0, 12.0, ((2, 2),)),
        "token_ids": touch_ends(jax.random.randint(part_keys[6], (BRANCHES,), 0, CANDS), jax.random.fold_in(part_keys[6], 1), 0, CANDS - 1).astype(jnp.int32),
        "fork_pos": touch_ends(jax.random.randint(part_keys[7], (BRANCHES,), 1, N_CTX + 1), jax.random.fold_in(part_keys[7], 1), 1, N_CTX).astype(jnp.int32),
        "slot_map": jax.random.permutation(part_keys[8], BRANCHES).astype(jnp.int32),
    }


def pair_tables():
    left, right = np.triu_indices(HEAD)
    coef = np.where(left == right, 1.0, math.sqrt(2.0))
    return (jnp.asarray(left, jnp.int32), jnp.asarray(right, jnp.int32), jnp.asarray(coef, jnp.float32))

def expand(block, left, right, coef):
    wide = block.astype(jnp.float32)
    return (jnp.take(wide, left, axis=1) * jnp.take(wide, right, axis=1) * coef).astype(jnp.bfloat16)

def reference(queries, keys, values, log_gate, cand_q, cand_kv, token_ids, fork_pos, slot_map):
    left, right, coef = pair_tables()
    highest = lax.Precision.HIGHEST
    spans = CONTEXT_LENGTH // TOK_DEV
    q_blocks = queries.reshape(spans, TOK_DEV, QHEADS * HEAD)
    k_blocks = keys.reshape(spans, TOK_DEV, LOOKUP_GROUPS * HEAD)
    v_blocks = values.reshape(spans, TOK_DEV, LOOKUP_GROUPS * HEAD)
    g_blocks = log_gate.reshape(spans, TOK_DEV, LOOKUP_GROUPS)
    new_q = cand_q[token_ids]
    new_k = cand_kv[token_ids, 0]
    new_v = cand_kv[token_ids, 1]
    phi_new = [expand(new_q[:, g * HEAD:(g + 1) * HEAD], left, right, coef).astype(jnp.float32) for g in range(QHEADS)]
    rowpos = lax.broadcasted_iota(jnp.int32, (TOK_DEV, TOK_DEV), 0)
    colpos = lax.broadcasted_iota(jnp.int32, (TOK_DEV, TOK_DEV), 1)
    causal = colpos <= rowpos

    def span_step(carry, inputs):
        states, norms, dec_num, dec_den = carry
        q_blk, k_blk, v_blk, g_blk, index = inputs
        cumul = jnp.cumsum(g_blk, axis=0)
        finals = cumul[-1]
        carry_w = jnp.exp(finals[None, :] - cumul)
        chosen = (fork_pos - 1 == index).astype(jnp.float32)
        outs = []
        next_states = []
        next_norms = []
        dnum_list = []
        dden_list = []
        for head in range(LOOKUP_GROUPS):
            key_h = k_blk[:, head * HEAD:(head + 1) * HEAD]
            value_h = v_blk[:, head * HEAD:(head + 1) * HEAD]
            phik = expand(key_h, left, right, coef).astype(jnp.float32)
            scaled = (carry_w[:, head:head + 1] * value_h.astype(jnp.float32)).astype(jnp.bfloat16).astype(jnp.float32)
            local_s = jnp.dot(phik.T, scaled, precision=highest)
            local_z = jnp.dot(carry_w[:, head].astype(jnp.bfloat16).astype(jnp.float32), phik, precision=highest)
            prior_s = states[head].astype(jnp.bfloat16).astype(jnp.float32)
            prior_z = norms[head].astype(jnp.bfloat16).astype(jnp.float32)
            growth = jnp.exp(cumul[:, head])
            spread = cumul[:, head][:, None] - cumul[:, head][None, :]
            fading = jnp.where(causal, jnp.exp(jnp.where(causal, spread, 0.0)), 0.0)
            incl_s = jnp.exp(finals[head]) * states[head] + local_s
            incl_z = jnp.exp(finals[head]) * norms[head] + local_z
            incl_sb = incl_s.astype(jnp.bfloat16).astype(jnp.float32)
            incl_zb = incl_z.astype(jnp.bfloat16).astype(jnp.float32)
            for member in range(GROUP):
                column = (head * GROUP + member) * HEAD
                q_h = q_blk[:, column:column + HEAD]
                phiq = expand(q_h, left, right, coef).astype(jnp.float32)
                inter_num = jnp.dot(phiq, prior_s, precision=highest) * growth[:, None] / HEAD
                inter_den = jnp.dot(phiq, prior_z, precision=highest) * growth / HEAD
                raw = jnp.dot(q_h, key_h.T, preferred_element_type=jnp.float32)
                weights = raw * raw / HEAD * fading
                numer = inter_num + jnp.dot(weights.astype(jnp.bfloat16), value_h, preferred_element_type=jnp.float32)
                denom = inter_den + lax.optimization_barrier(jnp.sum(weights, axis=1))
                outs.append((numer / jnp.maximum(denom, 1.0)[:, None]).astype(jnp.bfloat16))
                phin = phi_new[head * GROUP + member]
                dnum_list.append(jnp.dot(phin, incl_sb, precision=highest) * chosen[:, None] / HEAD)
                dden_list.append(jnp.dot(phin, incl_zb, precision=highest) * chosen / HEAD)
            next_states.append(incl_s)
            next_norms.append(incl_z)
        dec_num = dec_num + jnp.concatenate(dnum_list, axis=1)
        dec_den = dec_den + jnp.stack(dden_list, axis=1)
        return ((jnp.stack(next_states), jnp.stack(next_norms), dec_num, dec_den), jnp.concatenate(outs, axis=1))
    start = (jnp.zeros((LOOKUP_GROUPS, FEATS, HEAD), jnp.float32), jnp.zeros((LOOKUP_GROUPS, FEATS), jnp.float32), jnp.zeros((BRANCHES, QHEADS * HEAD), jnp.float32), jnp.zeros((BRANCHES, QHEADS), jnp.float32))
    indices = jnp.arange(spans).astype(jnp.int32)
    final, prefill = lax.scan(span_step, start, (q_blocks, k_blocks, v_blocks, g_blocks, indices))
    dec_num, dec_den = (final[2], final[3])
    pieces = []
    for head in range(LOOKUP_GROUPS):
        key_n = new_k[:, head * HEAD:(head + 1) * HEAD].astype(jnp.float32)
        value_n = new_v[:, head * HEAD:(head + 1) * HEAD].astype(jnp.float32)
        for member in range(GROUP):
            index = head * GROUP + member
            query_n = new_q[:, index * HEAD:(index + 1) * HEAD].astype(jnp.float32)
            inner = lax.optimization_barrier(jnp.sum(query_n * key_n, axis=1))
            own = inner * inner / HEAD
            numer = dec_num[:, index * HEAD:(index + 1) * HEAD] + own[:, None] * value_n
            denom = dec_den[:, index] + own
            pieces.append((numer / jnp.maximum(denom, 1.0)[:, None]).astype(jnp.bfloat16))
    ordered = jnp.concatenate(pieces, axis=1)
    branch_out = jnp.zeros((BRANCHES, QHEADS * HEAD), jnp.bfloat16).at[slot_map].set(ordered)
    return (prefill.reshape(CONTEXT_LENGTH, QHEADS * HEAD), branch_out)
```

```python
import jax
import jax.numpy as jnp
from jax import lax
from jax.sharding import PartitionSpec as P

HEAD = 128
GROUP = 5


def per_device(queries, keys, values, log_gate, cand_q, cand_kv, token_ids, fork_pos, slot_map):
    n = lax.axis_size("ctx")
    feats = lax.axis_size("feat")
    me = lax.axis_index("ctx")
    feat = lax.axis_index("feat")
    length = queries.shape[0]
    kv = keys.shape[1] // HEAD
    tri = jnp.tril(jnp.ones((length, length), jnp.float32))
    cumul = jnp.dot(tri, log_gate, precision=lax.Precision.HIGHEST)
    finals = cumul[-1]
    carry = jnp.exp(finals[None, :] - cumul)
    scaled = (
        (carry[:, :, None] * values.reshape(length, kv, HEAD).astype(jnp.float32))
        .astype(jnp.bfloat16)
        .reshape(length, kv * HEAD)
    )
    both = lax.all_gather(jnp.concatenate([keys, scaled], axis=1), "ctx")
    gates = lax.all_gather(cumul, "ctx")
    ends = gates[:, -1, :]
    carries = jnp.exp(ends[:, None, :] - gates)
    rows = length // feats
    start = feat * rows
    q = lax.dynamic_slice_in_dim(queries, start, rows, 0)
    own_cum = lax.dynamic_slice_in_dim(cumul, start, rows, 0)
    causal = (
        lax.broadcasted_iota(jnp.int32, (rows, length), 1)
        <= start + lax.broadcasted_iota(jnp.int32, (rows, length), 0)
    )
    branches = token_ids.shape[0]
    per = branches // (n * feats)
    first = (me * feats + feat) * per
    mine = (first + jnp.arange(per))[:, None] == slot_map[None, :]
    ids = jnp.sum(jnp.where(mine, token_ids[None, :], 0), axis=1)
    forks = jnp.sum(jnp.where(mine, fork_pos[None, :], 0), axis=1)
    pick = (ids[:, None] == jnp.arange(cand_q.shape[0])[None, :]).astype(jnp.bfloat16)
    new_q = jnp.dot(pick, cand_q, preferred_element_type=jnp.float32).astype(jnp.bfloat16)
    new_kv = jnp.einsum("rc,cpd->rpd", pick, cand_kv, preferred_element_type=jnp.float32)
    blocks = jnp.arange(n)

    def between(stop):
        inside = (blocks[None, :] > blocks[:, None]) & (blocks[None, :] < stop)
        total = jnp.sum(jnp.where(inside[:, :, None], ends[None], 0.0), axis=1)
        return jnp.where((blocks < stop)[:, None], jnp.exp(total), 0.0)

    fade_q = between(me)
    fade_b = jnp.stack([between(forks[i]) for i in range(per)])
    outs, bouts = [], []
    for h in range(kv):
        k_own = keys[:, h * HEAD : (h + 1) * HEAD]
        v_own = values[:, h * HEAD : (h + 1) * HEAD]
        k_all = both[:, :, h * HEAD : (h + 1) * HEAD]
        v_all = both[:, :, (kv + h) * HEAD : (kv + h + 1) * HEAD]
        qs = q[:, h * GROUP * HEAD : (h + 1) * GROUP * HEAD].reshape(rows, GROUP, HEAD)
        nq = new_q[:, h * GROUP * HEAD : (h + 1) * GROUP * HEAD].reshape(per, GROUP, HEAD)
        raw = jnp.einsum("tmd,bsd->btms", qs, k_all, preferred_element_type=jnp.float32)
        w = raw * raw
        num = jnp.einsum(
            "btms,bsd->btmd", w.astype(jnp.bfloat16), v_all, preferred_element_type=jnp.float32
        )
        den = jnp.sum(w * carries[:, None, None, :, h], axis=-1)
        growth = jnp.exp(own_cum[:, h])
        a = jnp.sum(num * fade_q[:, None, None, None, h], axis=0) * growth[:, None, None]
        b = jnp.sum(den * fade_q[:, None, None, h], axis=0) * growth[:, None]
        spread = own_cum[:, h][:, None] - cumul[:, h][None, :]
        fading = jnp.where(causal, jnp.exp(jnp.where(causal, spread, 0.0)), 0.0)
        raw = jnp.einsum("tmd,sd->tms", qs, k_own, preferred_element_type=jnp.float32)
        w = raw * raw * fading[:, None, :]
        a = a + jnp.einsum(
            "tms,sd->tmd", w.astype(jnp.bfloat16), v_own, preferred_element_type=jnp.float32
        )
        b = b + jnp.sum(w, axis=-1)
        outs.append(
            (a / HEAD / jnp.maximum(b / HEAD, 1.0)[:, :, None])
            .astype(jnp.bfloat16)
            .reshape(rows, GROUP * HEAD)
        )
        raw = jnp.einsum("rmd,bsd->brms", nq, k_all, preferred_element_type=jnp.float32)
        w = raw * raw
        num = jnp.einsum(
            "brms,bsd->brmd", w.astype(jnp.bfloat16), v_all, preferred_element_type=jnp.float32
        )
        den = jnp.sum(w * carries[:, None, None, :, h], axis=-1)
        fb = fade_b[:, :, h].T
        nk = new_kv[:, 0, h * HEAD : (h + 1) * HEAD].astype(jnp.float32)
        nv = new_kv[:, 1, h * HEAD : (h + 1) * HEAD].astype(jnp.float32)
        inner = jnp.sum(nq.astype(jnp.float32) * nk[:, None, :], axis=-1)
        u = inner * inner
        num = jnp.sum(num * fb[:, :, None, None], axis=0) + u[:, :, None] * nv[:, None, :]
        den = jnp.sum(den * fb[:, :, None], axis=0) + u
        bouts.append(
            (num / HEAD / jnp.maximum(den / HEAD, 1.0)[:, :, None])
            .astype(jnp.bfloat16)
            .reshape(per, GROUP * HEAD)
        )
    return jnp.concatenate(outs, axis=1), jnp.concatenate(bouts, axis=1)


def solution(mesh):
    return jax.shard_map(
        per_device,
        mesh=mesh,
        in_specs=(
            P(("groups", "ctx"), "head"),
            P(("groups", "ctx"), "head"),
            P(("groups", "ctx"), "head"),
            P(("groups", "ctx"), "head"),
            P("groups", "head"),
            P("groups", None, "head"),
            P("groups"),
            P("groups"),
            P("groups"),
        ),
        out_specs=(P(("groups", "ctx", "feat"), "head"), P(("groups", "ctx", "feat"), "head")),
        check_vma=False,
    )
```

```python
import functools

import jax
import jax.numpy as jnp
from jax import lax
from jax.experimental import pallas as pl
from jax.experimental.pallas import tpu as pltpu
from jax.sharding import PartitionSpec as P

HEAD = 128
GROUP = 5
F32, BF16 = jnp.float32, jnp.bfloat16
MESH = pl.DeviceIdType.MESH


def dot_t(a, b, **kw):
    return lax.dot_general(a, b, (((1,), (1,)), ((), ())), preferred_element_type=F32, **kw)


def kernel(
    n, feats, q_ref, k_ref, v_ref, g_ref, cq_ref, ckv_ref, ids_ref, fork_ref, slot_ref,
    out_ref, bout_ref, buf, gbuf, gcol, num, den, bscr,
    g_send, g_recv, z_send, z_recv, s_send, s_recv,
):
    me, feat = lax.axis_index("ctx"), lax.axis_index("feat")
    length = q_ref.shape[0]
    rows = length // feats
    kv = k_ref.shape[1] // HEAD
    start = pl.multiple_of(feat * rows, rows)
    count = ids_ref.shape[0]
    per = count // (n * feats)
    tall, wide = GROUP * rows, 8 * per

    barrier = pltpu.get_barrier_semaphore()
    for d in range(1, n):
        pl.semaphore_signal(
            barrier, inc=1, device_id={"ctx": lax.rem(me + d, n)}, device_id_type=MESH
        )
    for o in range(1, feats):
        pl.semaphore_signal(
            barrier, inc=1, device_id={"feat": lax.rem(feat + o, feats)}, device_id_type=MESH
        )

    r = lax.broadcasted_iota(jnp.int32, (length, length), 0)
    c = lax.broadcasted_iota(jnp.int32, (length, length), 1)
    tri = (c <= r).astype(F32)
    gates = g_ref[...]
    g_lane = dot_t(gates, tri, precision=lax.Precision.HIGHEST)
    g_row = dot_t(tri, gates, precision=lax.Precision.HIGHEST)
    gcol[...] = g_row
    gbuf[me] = jnp.zeros(gbuf.shape[1:], F32)
    gbuf[me, 0:kv, :] = g_lane
    carry = jnp.exp(g_row[length - 1 : length, :] - g_row)
    buf[me, 0] = k_ref[...]
    for h in range(kv):
        cols = slice(h * HEAD, (h + 1) * HEAD)
        buf[me, 1, :, cols] = (carry[:, h : h + 1] * v_ref[:, cols].astype(F32)).astype(BF16)

    pl.semaphore_wait(barrier, n - 1 + feats - 1)
    sends, gsends = [], []
    for d in range(1, n):
        there = {"ctx": lax.rem(me + d, n)}
        gsends.append(
            pltpu.make_async_remote_copy(
                src_ref=gbuf.at[me], dst_ref=gbuf.at[me], send_sem=g_send.at[d - 1],
                recv_sem=g_recv.at[d - 1], device_id=there, device_id_type=MESH,
            )
        )
        gsends[-1].start()
    for d in range(1, n):
        there = {"ctx": lax.rem(me + d, n)}
        part = buf.at[me, :, pl.ds(start, rows), :]
        sends.append(
            pltpu.make_async_remote_copy(
                src_ref=part, dst_ref=part, send_sem=z_send.at[d - 1],
                recv_sem=z_recv.at[d - 1], device_id=there, device_id_type=MESH,
            )
        )
        sends[-1].start()

    first = (me * feats + feat) * per
    ids, forks = [], []
    for i in range(per):
        a = b = jnp.int32(0)
        for s in range(count):
            hit = slot_ref[s] == first + i
            a = a + jnp.where(hit, ids_ref[s], 0)
            b = b + jnp.where(hit, fork_ref[s], 0)
        ids.append(a)
        forks.append(b)
    cands = cq_ref.shape[0]
    line = lax.broadcasted_iota(jnp.int32, (wide, cands), 0)
    place = lax.broadcasted_iota(jnp.int32, (wide, cands), 1)
    wanted = jnp.zeros((wide, cands), jnp.int32)
    brow = lax.broadcasted_iota(jnp.int32, (wide, 1), 0)
    stop = jnp.zeros((wide, 1), jnp.int32)
    for i in range(per):
        wanted = jnp.where(line >= 8 * i, ids[i], wanted)
        stop = jnp.where(brow >= 8 * i, forks[i], stop)
    pick = jnp.where(place == wanted, 1.0, 0.0).astype(BF16)
    new_kv = [ckv_ref[ids[i]].astype(F32) for i in range(per)]
    member = lax.broadcasted_iota(jnp.int32, (wide, HEAD), 0) % 8

    own_g = gcol[pl.ds(start, rows), :]
    t_at = start + lax.broadcasted_iota(jnp.int32, (rows, length), 0)
    causal = lax.broadcasted_iota(jnp.int32, (rows, length), 1) <= t_at
    stacked, new_q = [], []
    for h in range(kv):
        cols = slice(h * HEAD, (h + 1) * HEAD)
        base = h * GROUP * HEAD
        qs = jnp.concatenate(
            [q_ref[pl.ds(start, rows), base + m * HEAD : base + (m + 1) * HEAD] for m in range(GROUP)],
            axis=0,
        )
        nq = jnp.zeros((wide, HEAD), F32)
        for m in range(GROUP):
            got = jnp.dot(
                pick, cq_ref[:, base + m * HEAD : base + (m + 1) * HEAD], preferred_element_type=F32
            )
            nq = jnp.where(member == m, got, nq)
        new_q.append(nq)
        stacked.append(jnp.concatenate([qs, nq.astype(BF16)], axis=0))
        fading = jnp.where(
            causal,
            jnp.exp(jnp.where(causal, own_g[:, h : h + 1] - g_lane[h : h + 1, :], 0.0)),
            0.0,
        )
        raw = dot_t(qs, k_ref[:, cols])
        w = raw * raw * jnp.concatenate([fading] * GROUP, axis=0)
        num[h, 0:tall, :] = jnp.dot(w.astype(BF16), v_ref[:, cols], preferred_element_type=F32)
        den[h, 0:tall, :] = w
        nk = jnp.concatenate(
            [jnp.broadcast_to(x[0:1, cols], (8, HEAD)) for x in new_kv], axis=0
        )
        nv = jnp.concatenate(
            [jnp.broadcast_to(x[1:2, cols], (8, HEAD)) for x in new_kv], axis=0
        )
        inner = jnp.sum(nq * nk, axis=1, keepdims=True)
        u = inner * inner
        num[h, tall : tall + wide, :] = u * nv
        den[h, tall : tall + wide, :] = jnp.broadcast_to(u * (1.0 / HEAD), (wide, HEAD))

    for copy in gsends:
        copy.wait_recv()

    def decays(src, h):
        total_q = jnp.zeros((1, 1), F32)
        total_b = jnp.zeros((wide, 1), F32)
        for j in range(1, n):
            end = gbuf[j, h : h + 1, length - 1 : length]
            after = jnp.where(j > src, end, jnp.zeros_like(end))
            total_q = total_q + jnp.where(j < me, after, jnp.zeros_like(after))
            total_b = total_b + jnp.where(stop > j, after, 0.0)
        fade_q = jnp.exp(total_q) * jnp.where(src < me, 1.0, 0.0)
        fade_b = jnp.where(stop > src, jnp.exp(total_b), 0.0)
        return fade_q, fade_b

    def add(src, h, own):
        cols = slice(h * HEAD, (h + 1) * HEAD)
        fade_q, fade_b = decays(src, h)
        lanes = gbuf[src, h : h + 1, :]
        keep = jnp.exp(lanes[:, length - 1 : length] - lanes)
        lhs = new_q[h].astype(BF16) if own else stacked[h]
        raw = dot_t(lhs, buf[src, 0, :, cols])
        w = raw * raw
        got = jnp.dot(w.astype(BF16), buf[src, 1, :, cols], preferred_element_type=F32)
        w = w * keep
        if own:
            num[h, tall : tall + wide, :] += fade_b * got
            den[h, tall : tall + wide, :] += fade_b * w
            return
        grow = jnp.exp(own_g[:, h : h + 1]) * fade_q
        weight = jnp.concatenate([grow] * GROUP + [fade_b], axis=0)
        num[h] += weight * got
        den[h] += weight * w

    for h in range(kv):
        add(me, h, True)

    passed = []
    for d in range(1, n):
        src = lax.rem(me - d + n, n)
        sends[d - 1].wait_recv()
        part = buf.at[src, :, pl.ds(start, rows), :]
        hops = []
        for o in range(1, feats):
            copy = pltpu.make_async_remote_copy(
                src_ref=part, dst_ref=part, send_sem=s_send.at[d - 1, o - 1],
                recv_sem=s_recv.at[d - 1, o - 1],
                device_id={"feat": lax.rem(feat + o, feats)}, device_id_type=MESH,
            )
            copy.start()
            hops.append(copy)
        passed += hops
        for copy in hops:
            copy.wait_recv()
        for h in range(kv):
            add(src, h, False)

    for h in range(kv):
        total = jnp.sum(den[h], axis=1, keepdims=True) * (1.0 / HEAD)
        res = num[h] * (1.0 / HEAD) / jnp.maximum(total, 1.0)
        base = h * GROUP * HEAD
        for m in range(GROUP):
            cols = slice(base + m * HEAD, base + (m + 1) * HEAD)
            out_ref[:, cols] = res[m * rows : (m + 1) * rows].astype(BF16)
            for i in range(per):
                at = tall + 8 * i + m
                bscr[i : i + 1, cols] = res[at : at + 1]
    bout_ref[...] = bscr[...].astype(BF16)
    for copy in gsends + sends + passed:
        copy.wait_send()


def per_device(queries, keys, values, log_gate, cand_q, cand_kv, token_ids, fork_pos, slot_map):
    n, feats = lax.axis_size("ctx"), lax.axis_size("feat")
    length, width = queries.shape
    kv = keys.shape[1] // HEAD
    rows = length // feats
    per = token_ids.shape[0] // (n * feats)
    tall = GROUP * rows + 8 * per
    vmem, smem = pl.BlockSpec(memory_space=pltpu.VMEM), pl.BlockSpec(memory_space=pltpu.SMEM)
    dma = pltpu.SemaphoreType.DMA
    return pl.pallas_call(
        functools.partial(kernel, n, feats),
        out_shape=(
            jax.ShapeDtypeStruct((rows, width), BF16),
            jax.ShapeDtypeStruct((per, width), BF16),
        ),
        in_specs=[vmem] * 6 + [smem] * 3,
        out_specs=(vmem, vmem),
        scratch_shapes=[
            pltpu.VMEM((n, 2, length, kv * HEAD), BF16),
            pltpu.VMEM((n, -(-kv // 8) * 8, length), F32),
            pltpu.VMEM((length, kv), F32),
            pltpu.VMEM((kv, tall, HEAD), F32),
            pltpu.VMEM((kv, tall, HEAD), F32),
            pltpu.VMEM((per, width), F32),
            dma((n - 1,)), dma((n - 1,)), dma((n - 1,)), dma((n - 1,)),
            dma((n - 1, feats - 1)), dma((n - 1, feats - 1)),
        ],
        compiler_params=pltpu.CompilerParams(
            collective_id=0, has_side_effects=True, vmem_limit_bytes=40 * 2**20
        ),
    )(queries, keys, values, log_gate.T, cand_q, cand_kv, token_ids, fork_pos, slot_map)


def solution(mesh):
    return jax.shard_map(
        per_device,
        mesh=mesh,
        in_specs=(
            P(("groups", "ctx"), "head"),
            P(("groups", "ctx"), "head"),
            P(("groups", "ctx"), "head"),
            P(("groups", "ctx"), "head"),
            P("groups", "head"),
            P("groups", None, "head"),
            P("groups"),
            P("groups"),
            P("groups"),
        ),
        out_specs=(P(("groups", "ctx", "feat"), "head"), P(("groups", "ctx", "feat"), "head")),
        check_vma=False,
    )
```

```python
import functools

import jax
import jax.numpy as jnp
from jax import lax
from jax.experimental import pallas as pl
from jax.experimental.pallas import tpu as pltpu
from jax.sharding import PartitionSpec as P

HEAD = 128
GROUP = 5
F32, BF16 = jnp.float32, jnp.bfloat16
MESH = pl.DeviceIdType.MESH


def dot_t(a, b, **kw):
    return lax.dot_general(a, b, (((1,), (1,)), ((), ())), preferred_element_type=F32, **kw)


def kernel(
    n, feats, q_hbm, k_hbm, v_hbm, g_hbm, cq_hbm, ckv_hbm, ids_hbm, fork_hbm, slot_hbm,
    out_ref, bout_ref, q_ref, v_ref, g_ref, cq_ref, ckv_ref, ids_ref, fork_ref, slot_ref,
    buf, gbuf, gcol, num, den, bscr,
    l_sem, g_send, g_recv, z_send, z_recv, s_send, s_recv,
):
    me, feat = lax.axis_index("ctx"), lax.axis_index("feat")
    length = q_hbm.shape[0]
    rows = length // feats
    kv = k_hbm.shape[1] // HEAD
    up, down = me < n - 1, me > 0
    start = pl.multiple_of(feat * rows, rows)
    count = ids_ref.shape[0]
    per = count // (n * feats)
    tall, wide = GROUP * rows, 8 * per

    barrier = pltpu.get_barrier_semaphore()
    for d in range(1, n):
        pl.semaphore_signal(
            barrier, inc=1, device_id={"ctx": lax.rem(me + d, n)}, device_id_type=MESH
        )
    for o in range(1, feats):
        pl.semaphore_signal(
            barrier, inc=1, device_id={"feat": lax.rem(feat + o, feats)}, device_id_type=MESH
        )

    loads = [
        pltpu.make_async_copy(src, dst, l_sem.at[i])
        for i, (src, dst) in enumerate(
            [
                (g_hbm, g_ref), (v_hbm, v_ref), (k_hbm, buf.at[me, 0]),
                (q_hbm.at[pl.ds(start, rows), :], q_ref), (cq_hbm, cq_ref), (ckv_hbm, ckv_ref),
                (ids_hbm, ids_ref), (fork_hbm, fork_ref), (slot_hbm, slot_ref),
            ]
        )
    ]
    for copy in loads:
        copy.start()
    loads[0].wait()
    r = lax.broadcasted_iota(jnp.int32, (length, length), 0)
    c = lax.broadcasted_iota(jnp.int32, (length, length), 1)
    tri = (c <= r).astype(F32)
    gates = g_ref[...]
    g_lane = dot_t(gates, tri, precision=lax.Precision.HIGHEST)
    g_row = dot_t(tri, gates, precision=lax.Precision.HIGHEST)
    gcol[...] = g_row
    gbuf[me] = jnp.zeros(gbuf.shape[1:], F32)
    gbuf[me, 0:kv, :] = g_lane
    carry = jnp.exp(g_row[length - 1 : length, :] - g_row)
    def along(side, d, part):
        block = me - (d - 1) if side == 0 else me + (d - 1)
        ref = buf.at[block, part, pl.ds(start, rows), :]
        at = (side * (n - 1) + d - 1) * 2 + part
        return pltpu.make_async_remote_copy(
            src_ref=ref, dst_ref=ref, send_sem=z_send.at[at], recv_sem=z_recv.at[at],
            device_id={"ctx": me + 1 if side == 0 else me - 1}, device_id_type=MESH,
        )

    def arrival(side, d, part):
        block = me - d if side == 0 else me + d
        ref = buf.at[block, part, pl.ds(start, rows), :]
        at = (side * (n - 1) + d - 1) * 2 + part
        return pltpu.make_async_remote_copy(
            src_ref=ref, dst_ref=ref, send_sem=z_send.at[at], recv_sem=z_recv.at[at],
            device_id={"ctx": me - 1 if side == 0 else me + 1}, device_id_type=MESH,
        )

    def across(side, d, part):
        block = me - d if side == 0 else me + d
        ref = buf.at[block, part, pl.ds(start, rows), :]
        at = ((side * (n - 1) + d - 1) * 2 + part) * (feats - 1)
        return [
            pltpu.make_async_remote_copy(
                src_ref=ref, dst_ref=ref, send_sem=s_send.at[at + o - 1],
                recv_sem=s_recv.at[at + o - 1],
                device_id={"feat": lax.rem(feat + o, feats)}, device_id_type=MESH,
            )
            for o in range(1, feats)
        ]

    def sends(side, d):
        return (up if side == 0 else down) & arrives(side, d - 1)

    def arrives(side, d):
        return me >= d if side == 0 else me + d < n

    loads[2].wait()
    pl.semaphore_wait(barrier, n - 1 + feats - 1)
    gsends = []
    for d in range(1, n):
        there = {"ctx": lax.rem(me + d, n)}
        gsends.append(
            pltpu.make_async_remote_copy(
                src_ref=gbuf.at[me], dst_ref=gbuf.at[me], send_sem=g_send.at[d - 1],
                recv_sem=g_recv.at[d - 1], device_id=there, device_id_type=MESH,
            )
        )
        gsends[-1].start()
    for side in range(2):
        @pl.when(sends(side, 1))
        def _(side=side):
            along(side, 1, 0).start()
    loads[1].wait()
    for h in range(kv):
        cols = slice(h * HEAD, (h + 1) * HEAD)
        buf[me, 1, :, cols] = (carry[:, h : h + 1] * v_ref[:, cols].astype(F32)).astype(BF16)
    for side in range(2):
        @pl.when(sends(side, 1))
        def _(side=side):
            along(side, 1, 1).start()
    for copy in loads[3:]:
        copy.wait()

    first = (me * feats + feat) * per
    ids, forks = [], []
    for i in range(per):
        a = b = jnp.int32(0)
        for s in range(count):
            hit = slot_ref[s] == first + i
            a = a + jnp.where(hit, ids_ref[s], 0)
            b = b + jnp.where(hit, fork_ref[s], 0)
        ids.append(a)
        forks.append(b)
    cands = cq_ref.shape[0]
    line = lax.broadcasted_iota(jnp.int32, (wide, cands), 0)
    place = lax.broadcasted_iota(jnp.int32, (wide, cands), 1)
    wanted = jnp.zeros((wide, cands), jnp.int32)
    brow = lax.broadcasted_iota(jnp.int32, (wide, 1), 0)
    stop = jnp.zeros((wide, 1), jnp.int32)
    for i in range(per):
        wanted = jnp.where(line >= 8 * i, ids[i], wanted)
        stop = jnp.where(brow >= 8 * i, forks[i], stop)
    pick = jnp.where(place == wanted, 1.0, 0.0).astype(BF16)
    new_kv = [ckv_ref[ids[i]].astype(F32) for i in range(per)]
    member = lax.broadcasted_iota(jnp.int32, (wide, HEAD), 0) % 8

    own_g = gcol[pl.ds(start, rows), :]
    t_at = start + lax.broadcasted_iota(jnp.int32, (rows, length), 0)
    causal = lax.broadcasted_iota(jnp.int32, (rows, length), 1) <= t_at
    stacked, new_q = [], []
    for h in range(kv):
        cols = slice(h * HEAD, (h + 1) * HEAD)
        base = h * GROUP * HEAD
        qs = jnp.concatenate(
            [q_ref[:, base + m * HEAD : base + (m + 1) * HEAD] for m in range(GROUP)],
            axis=0,
        )
        nq = jnp.zeros((wide, HEAD), F32)
        for m in range(GROUP):
            got = jnp.dot(
                pick, cq_ref[:, base + m * HEAD : base + (m + 1) * HEAD], preferred_element_type=F32
            )
            nq = jnp.where(member == m, got, nq)
        new_q.append(nq)
        stacked.append(jnp.concatenate([qs, nq.astype(BF16)], axis=0))
        fading = jnp.where(
            causal,
            jnp.exp(jnp.where(causal, own_g[:, h : h + 1] - g_lane[h : h + 1, :], 0.0)),
            0.0,
        )
        raw = dot_t(qs, buf[me, 0, :, cols])
        w = raw * raw * jnp.concatenate([fading] * GROUP, axis=0)
        num[h, 0:tall, :] = jnp.dot(w.astype(BF16), v_ref[:, cols], preferred_element_type=F32)
        den[h, 0:tall, :] = w
        nk = jnp.concatenate(
            [jnp.broadcast_to(x[0:1, cols], (8, HEAD)) for x in new_kv], axis=0
        )
        nv = jnp.concatenate(
            [jnp.broadcast_to(x[1:2, cols], (8, HEAD)) for x in new_kv], axis=0
        )
        inner = jnp.sum(nq * nk, axis=1, keepdims=True)
        u = inner * inner
        num[h, tall : tall + wide, :] = u * nv
        den[h, tall : tall + wide, :] = jnp.broadcast_to(u * (1.0 / HEAD), (wide, HEAD))

    for copy in gsends:
        copy.wait_recv()

    def decays(src, h):
        total_q = jnp.zeros((1, 1), F32)
        total_b = jnp.zeros((wide, 1), F32)
        for j in range(1, n):
            end = gbuf[j, h : h + 1, length - 1 : length]
            after = jnp.where(j > src, end, jnp.zeros_like(end))
            total_q = total_q + jnp.where(j < me, after, jnp.zeros_like(after))
            total_b = total_b + jnp.where(stop > j, after, 0.0)
        fade_q = jnp.exp(total_q) * jnp.where(src < me, 1.0, 0.0)
        fade_b = jnp.where(stop > src, jnp.exp(total_b), 0.0)
        return fade_q, fade_b

    def add(src, h, own=False):
        cols = slice(h * HEAD, (h + 1) * HEAD)
        fade_q, fade_b = decays(src, h)
        lanes = gbuf[src, h : h + 1, :]
        keep = jnp.exp(lanes[:, length - 1 : length] - lanes)
        lhs = new_q[h].astype(BF16) if own else stacked[h]
        raw = dot_t(lhs, buf[src, 0, :, cols])
        w = raw * raw
        got = jnp.dot(w.astype(BF16), buf[src, 1, :, cols], preferred_element_type=F32)
        w = w * keep
        if own:
            num[h, tall : tall + wide, :] += fade_b * got
            den[h, tall : tall + wide, :] += fade_b * w
            return
        grow = jnp.exp(own_g[:, h : h + 1]) * fade_q
        weight = jnp.concatenate([grow] * GROUP + [fade_b], axis=0)
        num[h] += weight * got
        den[h] += weight * w

    for h in range(kv):
        add(me, h, True)

    for d in range(1, n):
        for side in range(2):
            @pl.when(arrives(side, d))
            def _(side=side, d=d):
                for part in range(2):
                    arrival(side, d, part).wait_recv()
                    if d < n - 1:
                        @pl.when(sends(side, d + 1))
                        def _():
                            along(side, d + 1, part).start()
                    for copy in across(side, d, part):
                        copy.start()
        for side in range(2):
            @pl.when(arrives(side, d))
            def _(side=side, d=d):
                for part in range(2):
                    for copy in across(side, d, part):
                        copy.wait_recv()
                for h in range(kv):
                    add(me - d if side == 0 else me + d, h, side == 1)

    for h in range(kv):
        total = jnp.sum(den[h], axis=1, keepdims=True) * (1.0 / HEAD)
        res = num[h] * (1.0 / HEAD) / jnp.maximum(total, 1.0)
        base = h * GROUP * HEAD
        for m in range(GROUP):
            cols = slice(base + m * HEAD, base + (m + 1) * HEAD)
            out_ref[:, cols] = res[m * rows : (m + 1) * rows].astype(BF16)
            for i in range(per):
                at = tall + 8 * i + m
                bscr[i : i + 1, cols] = res[at : at + 1]
    bout_ref[...] = bscr[...].astype(BF16)
    for copy in gsends:
        copy.wait_send()
    for d in range(1, n):
        for side in range(2):
            @pl.when(sends(side, d))
            def _(side=side, d=d):
                for part in range(2):
                    along(side, d, part).wait_send()

            @pl.when(arrives(side, d))
            def _(side=side, d=d):
                for part in range(2):
                    for copy in across(side, d, part):
                        copy.wait_send()


def per_device(queries, keys, values, log_gate, cand_q, cand_kv, token_ids, fork_pos, slot_map):
    n, feats = lax.axis_size("ctx"), lax.axis_size("feat")
    length, width = queries.shape
    kv = keys.shape[1] // HEAD
    rows = length // feats
    per = token_ids.shape[0] // (n * feats)
    tall = GROUP * rows + 8 * per
    vmem, hbm = pl.BlockSpec(memory_space=pltpu.VMEM), pl.BlockSpec(memory_space=pltpu.HBM)
    hops = 2 * (n - 1) * 2
    dma = pltpu.SemaphoreType.DMA
    return pl.pallas_call(
        functools.partial(kernel, n, feats),
        out_shape=(
            jax.ShapeDtypeStruct((rows, width), BF16),
            jax.ShapeDtypeStruct((per, width), BF16),
        ),
        in_specs=[hbm] * 9,
        out_specs=(vmem, vmem),
        scratch_shapes=[
            pltpu.VMEM((rows, width), BF16),
            pltpu.VMEM(values.shape, BF16),
            pltpu.VMEM((kv, length), F32),
            pltpu.VMEM(cand_q.shape, BF16),
            pltpu.VMEM(cand_kv.shape, BF16),
            pltpu.SMEM(token_ids.shape, jnp.int32),
            pltpu.SMEM(fork_pos.shape, jnp.int32),
            pltpu.SMEM(slot_map.shape, jnp.int32),
            pltpu.VMEM((n, 2, length, kv * HEAD), BF16),
            pltpu.VMEM((n, -(-kv // 8) * 8, length), F32),
            pltpu.VMEM((length, kv), F32),
            pltpu.VMEM((kv, tall, HEAD), F32),
            pltpu.VMEM((kv, tall, HEAD), F32),
            pltpu.VMEM((per, width), F32),
            dma((9,)), dma((n - 1,)), dma((n - 1,)), dma((hops,)), dma((hops,)),
            dma((hops * (feats - 1),)), dma((hops * (feats - 1),)),
        ],
        compiler_params=pltpu.CompilerParams(
            collective_id=0, has_side_effects=True, vmem_limit_bytes=40 * 2**20
        ),
    )(queries, keys, values, log_gate.T, cand_q, cand_kv, token_ids, fork_pos, slot_map)


def solution(mesh):
    return jax.shard_map(
        per_device,
        mesh=mesh,
        in_specs=(
            P(("groups", "ctx"), "head"),
            P(("groups", "ctx"), "head"),
            P(("groups", "ctx"), "head"),
            P(("groups", "ctx"), "head"),
            P("groups", "head"),
            P("groups", None, "head"),
            P("groups"),
            P("groups"),
            P("groups"),
        ),
        out_specs=(P(("groups", "ctx", "feat"), "head"), P(("groups", "ctx", "feat"), "head")),
        check_vma=False,
    )
```

```python
import functools

import jax
import jax.numpy as jnp
from jax import lax
from jax.experimental import pallas as pl
from jax.experimental.pallas import tpu as pltpu
from jax.sharding import PartitionSpec as P

HEAD = 128
GROUP = 5
F32, BF16 = jnp.float32, jnp.bfloat16
MESH = pl.DeviceIdType.MESH


def dot_t(a, b, **kw):
    return lax.dot_general(a, b, (((1,), (1,)), ((), ())), preferred_element_type=F32, **kw)


def kernel(
    n, feats, q_hbm, k_hbm, v_hbm, g_hbm, cq_hbm, ckv_hbm, ids_hbm, fork_hbm, slot_hbm,
    out_ref, bout_ref, q_ref, v_ref, g_ref, cq_ref, ckv_ref, ids_ref, fork_ref, slot_ref,
    buf, gbuf, gcol, num, den, bscr,
    l_sem, g_send, g_recv, z_send, z_recv, s_send, s_recv,
):
    me, feat = lax.axis_index("ctx"), lax.axis_index("feat")
    length = q_hbm.shape[0]
    rows = length // feats
    kv = k_hbm.shape[1] // HEAD
    up, down = me < n - 1, me > 0
    start = pl.multiple_of(feat * rows, rows)
    count = ids_ref.shape[0]
    per = count // (n * feats)
    tall, wide = GROUP * rows, 8 * per

    barrier = pltpu.get_barrier_semaphore()
    for d in range(1, n):
        pl.semaphore_signal(
            barrier, inc=1, device_id={"ctx": lax.rem(me + d, n)}, device_id_type=MESH
        )
    for o in range(1, feats):
        pl.semaphore_signal(
            barrier, inc=1, device_id={"feat": lax.rem(feat + o, feats)}, device_id_type=MESH
        )

    loads = [
        pltpu.make_async_copy(src, dst, l_sem.at[i])
        for i, (src, dst) in enumerate(
            [
                (g_hbm, g_ref), (v_hbm, v_ref), (k_hbm, buf.at[me, 0]),
                (q_hbm.at[pl.ds(start, rows), :], q_ref), (cq_hbm, cq_ref), (ckv_hbm, ckv_ref),
                (ids_hbm, ids_ref), (fork_hbm, fork_ref), (slot_hbm, slot_ref),
            ]
        )
    ]
    for copy in loads:
        copy.start()
    loads[0].wait()
    r = lax.broadcasted_iota(jnp.int32, (length, length), 0)
    c = lax.broadcasted_iota(jnp.int32, (length, length), 1)
    tri = (c <= r).astype(F32)
    gates = g_ref[...]
    g_lane = dot_t(gates, tri, precision=lax.Precision.HIGHEST)
    g_row = dot_t(tri, gates, precision=lax.Precision.HIGHEST)
    gcol[...] = g_row
    gbuf[me] = jnp.zeros(gbuf.shape[1:], F32)
    gbuf[me, 0:kv, :] = g_lane
    carry = jnp.exp(g_row[length - 1 : length, :] - g_row)
    def along(side, d, part):
        block = me - (d - 1) if side == 0 else me + (d - 1)
        ref = buf.at[block, part, pl.ds(start, rows), :]
        at = (side * (n - 1) + d - 1) * 2 + part
        return pltpu.make_async_remote_copy(
            src_ref=ref, dst_ref=ref, send_sem=z_send.at[at], recv_sem=z_recv.at[at],
            device_id={"ctx": me + 1 if side == 0 else me - 1}, device_id_type=MESH,
        )

    def arrival(side, d, part):
        block = me - d if side == 0 else me + d
        ref = buf.at[block, part, pl.ds(start, rows), :]
        at = (side * (n - 1) + d - 1) * 2 + part
        return pltpu.make_async_remote_copy(
            src_ref=ref, dst_ref=ref, send_sem=z_send.at[at], recv_sem=z_recv.at[at],
            device_id={"ctx": me - 1 if side == 0 else me + 1}, device_id_type=MESH,
        )

    def across(side, d, part):
        block = me - d if side == 0 else me + d
        ref = buf.at[block, part, pl.ds(start, rows), :]
        at = ((side * (n - 1) + d - 1) * 2 + part) * (feats - 1)
        return [
            pltpu.make_async_remote_copy(
                src_ref=ref, dst_ref=ref, send_sem=s_send.at[at + o - 1],
                recv_sem=s_recv.at[at + o - 1],
                device_id={"feat": lax.rem(feat + o, feats)}, device_id_type=MESH,
            )
            for o in range(1, feats)
        ]

    def sends(side, d):
        return (up if side == 0 else down) & arrives(side, d - 1)

    def arrives(side, d):
        return me >= d if side == 0 else me + d < n

    loads[2].wait()
    pl.semaphore_wait(barrier, n - 1 + feats - 1)
    gsends = []
    for d in range(1, n):
        there = {"ctx": lax.rem(me + d, n)}
        gsends.append(
            pltpu.make_async_remote_copy(
                src_ref=gbuf.at[me], dst_ref=gbuf.at[me], send_sem=g_send.at[d - 1],
                recv_sem=g_recv.at[d - 1], device_id=there, device_id_type=MESH,
            )
        )
        gsends[-1].start()
    for side in range(2):
        @pl.when(sends(side, 1))
        def _(side=side):
            along(side, 1, 0).start()
    loads[1].wait()
    for h in range(kv):
        cols = slice(h * HEAD, (h + 1) * HEAD)
        buf[me, 1, :, cols] = (carry[:, h : h + 1] * v_ref[:, cols].astype(F32)).astype(BF16)
    for side in range(2):
        @pl.when(sends(side, 1))
        def _(side=side):
            along(side, 1, 1).start()
    for copy in loads[3:]:
        copy.wait()

    first = (me * feats + feat) * per
    ids, forks = [], []
    for i in range(per):
        a = b = jnp.int32(0)
        for s in range(count):
            hit = slot_ref[s] == first + i
            a = a + jnp.where(hit, ids_ref[s], 0)
            b = b + jnp.where(hit, fork_ref[s], 0)
        ids.append(a)
        forks.append(b)
    cands = cq_ref.shape[0]
    line = lax.broadcasted_iota(jnp.int32, (wide, cands), 0)
    place = lax.broadcasted_iota(jnp.int32, (wide, cands), 1)
    wanted = jnp.zeros((wide, cands), jnp.int32)
    brow = lax.broadcasted_iota(jnp.int32, (wide, 1), 0)
    stop = jnp.zeros((wide, 1), jnp.int32)
    for i in range(per):
        wanted = jnp.where(line >= 8 * i, ids[i], wanted)
        stop = jnp.where(brow >= 8 * i, forks[i], stop)
    pick = jnp.where(place == wanted, 1.0, 0.0).astype(BF16)
    new_kv = [ckv_ref[ids[i]].astype(F32) for i in range(per)]
    member = lax.broadcasted_iota(jnp.int32, (wide, HEAD), 0) % 8

    own_g = gcol[pl.ds(start, rows), :]
    t_at = start + lax.broadcasted_iota(jnp.int32, (rows, length), 0)
    causal = lax.broadcasted_iota(jnp.int32, (rows, length), 1) <= t_at
    stacked, new_q = [], []
    for h in range(kv):
        cols = slice(h * HEAD, (h + 1) * HEAD)
        base = h * GROUP * HEAD
        qs = jnp.concatenate(
            [q_ref[:, base + m * HEAD : base + (m + 1) * HEAD] for m in range(GROUP)],
            axis=0,
        )
        nq = jnp.zeros((wide, HEAD), F32)
        for m in range(GROUP):
            got = jnp.dot(
                pick, cq_ref[:, base + m * HEAD : base + (m + 1) * HEAD], preferred_element_type=F32
            )
            nq = jnp.where(member == m, got, nq)
        new_q.append(nq)
        stacked.append(jnp.concatenate([qs, nq.astype(BF16)], axis=0))
        fading = jnp.where(
            causal,
            jnp.exp(jnp.where(causal, own_g[:, h : h + 1] - g_lane[h : h + 1, :], 0.0)),
            0.0,
        )
        raw = dot_t(qs, buf[me, 0, :, cols])
        w = raw * raw * jnp.concatenate([fading] * GROUP, axis=0)
        num[h, 0:tall, :] = jnp.dot(w.astype(BF16), v_ref[:, cols], preferred_element_type=F32)
        den[h, 0:tall, :] = w
        nk = jnp.concatenate(
            [jnp.broadcast_to(x[0:1, cols], (8, HEAD)) for x in new_kv], axis=0
        )
        nv = jnp.concatenate(
            [jnp.broadcast_to(x[1:2, cols], (8, HEAD)) for x in new_kv], axis=0
        )
        inner = jnp.sum(nq * nk, axis=1, keepdims=True)
        u = inner * inner
        num[h, tall : tall + wide, :] = u * nv
        den[h, tall : tall + wide, :] = jnp.broadcast_to(u * (1.0 / HEAD), (wide, HEAD))

    for copy in gsends:
        copy.wait_recv()

    def decays(src, h):
        total_q = jnp.zeros((1, 1), F32)
        total_b = jnp.zeros((wide, 1), F32)
        for j in range(1, n):
            end = gbuf[j, h : h + 1, length - 1 : length]
            after = jnp.where(j > src, end, jnp.zeros_like(end))
            total_q = total_q + jnp.where(j < me, after, jnp.zeros_like(after))
            total_b = total_b + jnp.where(stop > j, after, 0.0)
        fade_q = jnp.exp(total_q) * jnp.where(src < me, 1.0, 0.0)
        fade_b = jnp.where(stop > src, jnp.exp(total_b), 0.0)
        return fade_q, fade_b

    def add(src, h, own=False):
        cols = slice(h * HEAD, (h + 1) * HEAD)
        fade_q, fade_b = decays(src, h)
        lanes = gbuf[src, h : h + 1, :]
        keep = jnp.exp(lanes[:, length - 1 : length] - lanes)
        lhs = new_q[h].astype(BF16) if own else stacked[h]
        raw = dot_t(lhs, buf[src, 0, :, cols])
        w = raw * raw
        got = jnp.dot(w.astype(BF16), buf[src, 1, :, cols], preferred_element_type=F32)
        w = w * keep
        if own:
            num[h, tall : tall + wide, :] += fade_b * got
            den[h, tall : tall + wide, :] += fade_b * w
            return
        grow = jnp.exp(own_g[:, h : h + 1]) * fade_q
        weight = jnp.concatenate([grow] * GROUP + [fade_b], axis=0)
        num[h] += weight * got
        den[h] += weight * w

    for h in range(kv):
        add(me, h, True)

    for d in range(1, n):
        for side in range(2):
            @pl.when(arrives(side, d))
            def _(side=side, d=d):
                for part in range(2):
                    arrival(side, d, part).wait_recv()
                    if d < n - 1:
                        @pl.when(sends(side, d + 1))
                        def _():
                            along(side, d + 1, part).start()
                    for copy in across(side, d, part):
                        copy.start()
        for side in range(2):
            @pl.when(arrives(side, d))
            def _(side=side, d=d):
                for part in range(2):
                    for copy in across(side, d, part):
                        copy.wait_recv()
                for h in range(kv):
                    add(me - d if side == 0 else me + d, h, side == 1)

    for h in range(kv):
        total = jnp.sum(den[h], axis=1, keepdims=True) * (1.0 / HEAD)
        res = num[h] * (1.0 / HEAD) / jnp.maximum(total, 1.0)
        base = h * GROUP * HEAD
        for m in range(GROUP):
            cols = slice(base + m * HEAD, base + (m + 1) * HEAD)
            out_ref[:, cols] = res[m * rows : (m + 1) * rows].astype(BF16)
            for i in range(per):
                at = tall + 8 * i + m
                bscr[i : i + 1, cols] = res[at : at + 1]
    bout_ref[...] = bscr[...].astype(BF16)
    for copy in gsends:
        copy.wait_send()
    for d in range(1, n):
        for side in range(2):
            @pl.when(sends(side, d))
            def _(side=side, d=d):
                for part in range(2):
                    along(side, d, part).wait_send()

            @pl.when(arrives(side, d))
            def _(side=side, d=d):
                for part in range(2):
                    for copy in across(side, d, part):
                        copy.wait_send()


def per_device(queries, keys, values, log_gate, cand_q, cand_kv, token_ids, fork_pos, slot_map):
    n, feats = lax.axis_size("ctx"), lax.axis_size("feat")
    length, width = queries.shape
    kv = keys.shape[1] // HEAD
    rows = length // feats
    per = token_ids.shape[0] // (n * feats)
    tall = GROUP * rows + 8 * per
    vmem, hbm = pl.BlockSpec(memory_space=pltpu.VMEM), pl.BlockSpec(memory_space=pltpu.HBM)
    hops = 2 * (n - 1) * 2
    dma = pltpu.SemaphoreType.DMA
    return pl.pallas_call(
        functools.partial(kernel, n, feats),
        out_shape=(
            jax.ShapeDtypeStruct((rows, width), BF16),
            jax.ShapeDtypeStruct((per, width), BF16),
        ),
        in_specs=[hbm] * 9,
        out_specs=(vmem, vmem),
        scratch_shapes=[
            pltpu.VMEM((rows, width), BF16),
            pltpu.VMEM(values.shape, BF16),
            pltpu.VMEM((kv, length), F32),
            pltpu.VMEM(cand_q.shape, BF16),
            pltpu.VMEM(cand_kv.shape, BF16),
            pltpu.SMEM(token_ids.shape, jnp.int32),
            pltpu.SMEM(fork_pos.shape, jnp.int32),
            pltpu.SMEM(slot_map.shape, jnp.int32),
            pltpu.VMEM((n, 2, length, kv * HEAD), BF16),
            pltpu.VMEM((n, -(-kv // 8) * 8, length), F32),
            pltpu.VMEM((length, kv), F32),
            pltpu.VMEM((kv, tall, HEAD), F32),
            pltpu.VMEM((kv, tall, HEAD), F32),
            pltpu.VMEM((per, width), F32),
            dma((9,)), dma((n - 1,)), dma((n - 1,)), dma((hops,)), dma((hops,)),
            dma((hops * (feats - 1),)), dma((hops * (feats - 1),)),
        ],
        compiler_params=pltpu.CompilerParams(
            collective_id=0, has_side_effects=True, vmem_limit_bytes=64 * 2**20 - 2**16
        ),
    )(queries, keys, values, log_gate.T, cand_q, cand_kv, token_ids, fork_pos, slot_map)


def solution(mesh):
    return jax.shard_map(
        per_device,
        mesh=mesh,
        in_specs=(
            P(("groups", "ctx"), "head"),
            P(("groups", "ctx"), "head"),
            P(("groups", "ctx"), "head"),
            P(("groups", "ctx"), "head"),
            P("groups", "head"),
            P("groups", None, "head"),
            P("groups"),
            P("groups"),
            P("groups"),
        ),
        out_specs=(P(("groups", "ctx", "feat"), "head"), P(("groups", "ctx", "feat"), "head")),
        check_vma=False,
    )
```

```python
import functools

import jax
import jax.numpy as jnp
from jax import lax
from jax.experimental import pallas as pl
from jax.experimental.pallas import tpu as pltpu
from jax.sharding import PartitionSpec as P

HEAD = 128
GROUP = 5
F32, BF16 = jnp.float32, jnp.bfloat16
MESH = pl.DeviceIdType.MESH


def dot_t(a, b, **kw):
    return lax.dot_general(a, b, (((1,), (1,)), ((), ())), preferred_element_type=F32, **kw)


def kernel(
    n, feats, q_hbm, k_hbm, v_hbm, g_hbm, cq_hbm, ckv_hbm, ids_hbm, fork_hbm, slot_hbm,
    out_ref, bout_ref, q_ref, v_ref, g_ref, cq_ref, ckv_ref, ids_ref, fork_ref, slot_ref,
    buf, gbuf, gcol, num, den, bscr,
    l_sem, g_send, g_recv, z_send, z_recv, s_send, s_recv,
):
    me, feat = lax.axis_index("ctx"), lax.axis_index("feat")
    length = q_hbm.shape[0]
    rows = length // feats
    kv = k_hbm.shape[1] // HEAD
    up, down = me < n - 1, me > 0
    start = pl.multiple_of(feat * rows, rows)
    count = ids_ref.shape[0]
    per = count // (n * feats)
    tall, wide = GROUP * rows, 8 * per

    barrier = pltpu.get_barrier_semaphore()
    for d in range(1, n):
        pl.semaphore_signal(
            barrier, inc=1, device_id={"ctx": lax.rem(me + d, n)}, device_id_type=MESH
        )
    for o in range(1, feats):
        pl.semaphore_signal(
            barrier, inc=1, device_id={"feat": lax.rem(feat + o, feats)}, device_id_type=MESH
        )

    loads = [
        pltpu.make_async_copy(src, dst, l_sem.at[i])
        for i, (src, dst) in enumerate(
            [
                (g_hbm, g_ref), (v_hbm, v_ref), (k_hbm, buf.at[me, 0]),
                (q_hbm.at[pl.ds(start, rows), :], q_ref), (cq_hbm, cq_ref), (ckv_hbm, ckv_ref),
                (ids_hbm, ids_ref), (fork_hbm, fork_ref), (slot_hbm, slot_ref),
            ]
        )
    ]
    for copy in loads:
        copy.start()
    loads[0].wait()
    r = lax.broadcasted_iota(jnp.int32, (length, length), 0)
    c = lax.broadcasted_iota(jnp.int32, (length, length), 1)
    tri = (c <= r).astype(F32)
    gates = g_ref[...]
    g_lane = dot_t(gates, tri, precision=lax.Precision.HIGHEST)
    g_row = dot_t(tri, gates, precision=lax.Precision.HIGHEST)
    gcol[...] = g_row
    gbuf[me] = jnp.zeros(gbuf.shape[1:], F32)
    gbuf[me, 0:kv, :] = g_lane
    carry = jnp.exp(g_row[length - 1 : length, :] - g_row)
    def along(side, d, part):
        block = me - (d - 1) if side == 0 else me + (d - 1)
        ref = buf.at[block, part, pl.ds(start, rows), :]
        at = (side * (n - 1) + d - 1) * 2 + part
        return pltpu.make_async_remote_copy(
            src_ref=ref, dst_ref=ref, send_sem=z_send.at[at], recv_sem=z_recv.at[at],
            device_id={"ctx": me + 1 if side == 0 else me - 1}, device_id_type=MESH,
        )

    def arrival(side, d, part):
        block = me - d if side == 0 else me + d
        ref = buf.at[block, part, pl.ds(start, rows), :]
        at = (side * (n - 1) + d - 1) * 2 + part
        return pltpu.make_async_remote_copy(
            src_ref=ref, dst_ref=ref, send_sem=z_send.at[at], recv_sem=z_recv.at[at],
            device_id={"ctx": me - 1 if side == 0 else me + 1}, device_id_type=MESH,
        )

    def across(side, d, part):
        block = me - d if side == 0 else me + d
        ref = buf.at[block, part, pl.ds(start, rows), :]
        at = ((side * (n - 1) + d - 1) * 2 + part) * (feats - 1)
        return [
            pltpu.make_async_remote_copy(
                src_ref=ref, dst_ref=ref, send_sem=s_send.at[at + o - 1],
                recv_sem=s_recv.at[at + o - 1],
                device_id={"feat": lax.rem(feat + o, feats)}, device_id_type=MESH,
            )
            for o in range(1, feats)
        ]

    def sends(side, d):
        return (up if side == 0 else down) & arrives(side, d - 1)

    def arrives(side, d):
        return me >= d if side == 0 else me + d < n

    loads[2].wait()
    pl.semaphore_wait(barrier, n - 1 + feats - 1)
    gsends = []
    for d in range(1, n):
        there = {"ctx": lax.rem(me + d, n)}
        gsends.append(
            pltpu.make_async_remote_copy(
                src_ref=gbuf.at[me], dst_ref=gbuf.at[me], send_sem=g_send.at[d - 1],
                recv_sem=g_recv.at[d - 1], device_id=there, device_id_type=MESH,
            )
        )
        gsends[-1].start()
    for side in range(2):
        @pl.when(sends(side, 1))
        def _(side=side):
            along(side, 1, 0).start()
    loads[1].wait()
    for h in range(kv):
        cols = slice(h * HEAD, (h + 1) * HEAD)
        buf[me, 1, :, cols] = (carry[:, h : h + 1] * v_ref[:, cols].astype(F32)).astype(BF16)
    for side in range(2):
        @pl.when(sends(side, 1))
        def _(side=side):
            along(side, 1, 1).start()
    for copy in loads[3:]:
        copy.wait()

    first = (me * feats + feat) * per
    ids, forks = [], []
    for i in range(per):
        a = b = jnp.int32(0)
        for s in range(count):
            hit = slot_ref[s] == first + i
            a = a + jnp.where(hit, ids_ref[s], 0)
            b = b + jnp.where(hit, fork_ref[s], 0)
        ids.append(a)
        forks.append(b)
    cands = cq_ref.shape[0]
    line = lax.broadcasted_iota(jnp.int32, (wide, cands), 0)
    place = lax.broadcasted_iota(jnp.int32, (wide, cands), 1)
    wanted = jnp.zeros((wide, cands), jnp.int32)
    brow = lax.broadcasted_iota(jnp.int32, (wide, 1), 0)
    stop = jnp.zeros((wide, 1), jnp.int32)
    for i in range(per):
        wanted = jnp.where(line >= 8 * i, ids[i], wanted)
        stop = jnp.where(brow >= 8 * i, forks[i], stop)
    pick = jnp.where(place == wanted, 1.0, 0.0).astype(BF16)
    new_kv = [ckv_ref[ids[i]].astype(F32) for i in range(per)]
    member = lax.broadcasted_iota(jnp.int32, (wide, HEAD), 0) % 8

    own_g = gcol[pl.ds(start, rows), :]
    t_at = start + lax.broadcasted_iota(jnp.int32, (rows, length), 0)
    causal = lax.broadcasted_iota(jnp.int32, (rows, length), 1) <= t_at
    stacked, new_q = [], []
    for h in range(kv):
        cols = slice(h * HEAD, (h + 1) * HEAD)
        base = h * GROUP * HEAD
        qs = jnp.concatenate(
            [q_ref[:, base + m * HEAD : base + (m + 1) * HEAD] for m in range(GROUP)],
            axis=0,
        )
        nq = jnp.zeros((wide, HEAD), F32)
        for m in range(GROUP):
            got = jnp.dot(
                pick, cq_ref[:, base + m * HEAD : base + (m + 1) * HEAD], preferred_element_type=F32
            )
            nq = jnp.where(member == m, got, nq)
        new_q.append(nq)
        stacked.append(jnp.concatenate([qs, nq.astype(BF16)], axis=0))
        fading = jnp.where(
            causal,
            jnp.exp(jnp.where(causal, own_g[:, h : h + 1] - g_lane[h : h + 1, :], 0.0)),
            0.0,
        )
        raw = dot_t(qs, buf[me, 0, :, cols])
        w = raw * raw * jnp.concatenate([fading] * GROUP, axis=0)
        num[h, 0:tall, :] = jnp.dot(w.astype(BF16), v_ref[:, cols], preferred_element_type=F32)
        den[h, 0:tall, :] = w
        nk = jnp.concatenate(
            [jnp.broadcast_to(x[0:1, cols], (8, HEAD)) for x in new_kv], axis=0
        )
        nv = jnp.concatenate(
            [jnp.broadcast_to(x[1:2, cols], (8, HEAD)) for x in new_kv], axis=0
        )
        inner = jnp.sum(nq * nk, axis=1, keepdims=True)
        u = inner * inner
        num[h, tall : tall + wide, :] = u * nv
        den[h, tall : tall + wide, :] = jnp.broadcast_to(u * (1.0 / HEAD), (wide, HEAD))

    for copy in gsends:
        copy.wait_recv()

    def decays(src, h):
        total_q = jnp.zeros((1, 1), F32)
        total_b = jnp.zeros((wide, 1), F32)
        for j in range(1, n):
            end = gbuf[j, h : h + 1, length - 1 : length]
            after = jnp.where(j > src, end, jnp.zeros_like(end))
            total_q = total_q + jnp.where(j < me, after, jnp.zeros_like(after))
            total_b = total_b + jnp.where(stop > j, after, 0.0)
        fade_q = jnp.exp(total_q) * jnp.where(src < me, 1.0, 0.0)
        fade_b = jnp.where(stop > src, jnp.exp(total_b), 0.0)
        return fade_q, fade_b

    def add(src, h, own=False):
        cols = slice(h * HEAD, (h + 1) * HEAD)
        fade_q, fade_b = decays(src, h)
        lanes = gbuf[src, h : h + 1, :]
        keep = jnp.exp(lanes[:, length - 1 : length] - lanes)
        lhs = new_q[h].astype(BF16) if own else stacked[h]
        raw = dot_t(lhs, buf[src, 0, :, cols])
        w = raw * raw
        got = jnp.dot(w.astype(BF16), buf[src, 1, :, cols], preferred_element_type=F32)
        w = w * keep
        if own:
            num[h, tall : tall + wide, :] += fade_b * got
            den[h, tall : tall + wide, :] += fade_b * w
            return
        grow = jnp.exp(own_g[:, h : h + 1]) * fade_q
        weight = jnp.concatenate([grow] * GROUP + [fade_b], axis=0)
        num[h] += weight * got
        den[h] += weight * w

    for h in range(kv):
        add(me, h, True)

    for d in range(1, n):
        for part in range(2):
            for side in range(2):
                @pl.when(arrives(side, d))
                def _(side=side, d=d, part=part):
                    arrival(side, d, part).wait_recv()
                    if d < n - 1:
                        @pl.when(sends(side, d + 1))
                        def _():
                            along(side, d + 1, part).start()
                    for copy in across(side, d, part):
                        copy.start()
        for side in range(2):
            @pl.when(arrives(side, d))
            def _(side=side, d=d):
                for part in range(2):
                    for copy in across(side, d, part):
                        copy.wait_recv()
                for h in range(kv):
                    add(me - d if side == 0 else me + d, h, side == 1)

    for h in range(kv):
        total = jnp.sum(den[h], axis=1, keepdims=True) * (1.0 / HEAD)
        res = num[h] * (1.0 / HEAD) / jnp.maximum(total, 1.0)
        base = h * GROUP * HEAD
        for m in range(GROUP):
            cols = slice(base + m * HEAD, base + (m + 1) * HEAD)
            out_ref[:, cols] = res[m * rows : (m + 1) * rows].astype(BF16)
            for i in range(per):
                at = tall + 8 * i + m
                bscr[i : i + 1, cols] = res[at : at + 1]
    bout_ref[...] = bscr[...].astype(BF16)
    for copy in gsends:
        copy.wait_send()
    for d in range(1, n):
        for side in range(2):
            @pl.when(sends(side, d))
            def _(side=side, d=d):
                for part in range(2):
                    along(side, d, part).wait_send()

            @pl.when(arrives(side, d))
            def _(side=side, d=d):
                for part in range(2):
                    for copy in across(side, d, part):
                        copy.wait_send()


def per_device(queries, keys, values, log_gate, cand_q, cand_kv, token_ids, fork_pos, slot_map):
    n, feats = lax.axis_size("ctx"), lax.axis_size("feat")
    length, width = queries.shape
    kv = keys.shape[1] // HEAD
    rows = length // feats
    per = token_ids.shape[0] // (n * feats)
    tall = GROUP * rows + 8 * per
    vmem, hbm = pl.BlockSpec(memory_space=pltpu.VMEM), pl.BlockSpec(memory_space=pltpu.HBM)
    hops = 2 * (n - 1) * 2
    dma = pltpu.SemaphoreType.DMA
    return pl.pallas_call(
        functools.partial(kernel, n, feats),
        out_shape=(
            jax.ShapeDtypeStruct((rows, width), BF16),
            jax.ShapeDtypeStruct((per, width), BF16),
        ),
        in_specs=[hbm] * 9,
        out_specs=(vmem, vmem),
        scratch_shapes=[
            pltpu.VMEM((rows, width), BF16),
            pltpu.VMEM(values.shape, BF16),
            pltpu.VMEM((kv, length), F32),
            pltpu.VMEM(cand_q.shape, BF16),
            pltpu.VMEM(cand_kv.shape, BF16),
            pltpu.SMEM(token_ids.shape, jnp.int32),
            pltpu.SMEM(fork_pos.shape, jnp.int32),
            pltpu.SMEM(slot_map.shape, jnp.int32),
            pltpu.VMEM((n, 2, length, kv * HEAD), BF16),
            pltpu.VMEM((n, -(-kv // 8) * 8, length), F32),
            pltpu.VMEM((length, kv), F32),
            pltpu.VMEM((kv, tall, HEAD), F32),
            pltpu.VMEM((kv, tall, HEAD), F32),
            pltpu.VMEM((per, width), F32),
            dma((9,)), dma((n - 1,)), dma((n - 1,)), dma((hops,)), dma((hops,)),
            dma((hops * (feats - 1),)), dma((hops * (feats - 1),)),
        ],
        compiler_params=pltpu.CompilerParams(
            collective_id=0, has_side_effects=True, vmem_limit_bytes=64 * 2**20 - 2**16
        ),
    )(queries, keys, values, log_gate.T, cand_q, cand_kv, token_ids, fork_pos, slot_map)


def solution(mesh):
    return jax.shard_map(
        per_device,
        mesh=mesh,
        in_specs=(
            P(("groups", "ctx"), "head"),
            P(("groups", "ctx"), "head"),
            P(("groups", "ctx"), "head"),
            P(("groups", "ctx"), "head"),
            P("groups", "head"),
            P("groups", None, "head"),
            P("groups"),
            P("groups"),
            P("groups"),
        ),
        out_specs=(P(("groups", "ctx", "feat"), "head"), P(("groups", "ctx", "feat"), "head")),
        check_vma=False,
    )
```
